32 devices in a mesh: chan: 16 (over z, x, core), win: 2 (over y).
Axes of the slice: x: 2, y: 2, z: 4, core: 2. Of those that a mesh axis runs over, the one named last changes fastest.
Arguments:
- traces: float32 [512, 4, 1024], P('chan', 'win'), may hold values from -100 to 100, as said below
- live_counts: int32 [16], P('chan'), may hold values from 1 to 32, as said below
- pair_lists: int32 [16, 4, 3], P('chan'), may hold values from 0 to 15, as said below
Outputs:
- correlations: float32 [1024, 64, 256], P('win', 'chan')
The draws below stay inside these ranges and needn't reach their ends.
Inputs may be any that keep to these rules, and one draw needn't show every extreme that they name: `traces`: sum of a random-amplitude noise, a band tone and an offset for each channel and sub-window. `live_counts`: at least one block has all 32 channels live. `pair_lists`: the valid slots of an owner come first, 1 to 4 of them, and some owner has all 4; in a valid slot the first block is at most the second; padded slots are (0, 0, 0).
All inputs are finite; a program needn't handle non-finite values.
Results may differ from the reference program's by a relative error of at most 0.000073.
Values sent between devices are 32-bit elements; how exact they have to be, the bound alone decides.
A program may use at most 128 MiB of HBM per device.

```python
import math
import jax
import jax.numpy as jnp
from jax import lax

CH = 32
SAMP = 1024
F0 = 2
NF = 128
NLAG = 256
PMAX = 4
CHANNELS = 512
WINDOWS = 4
N_CHAN = 16


def draw_traces(key, part):
    key = jax.random.fold_in(key, 11)
    keys = jax.random.split(key, 6)
    shape = (CHANNELS, WINDOWS, SAMP)
    small = (CHANNELS, WINDOWS, 1)
    scales = jnp.exp(jax.random.uniform(keys[0], small) * math.log(10.0))
    noise = jnp.clip(jax.random.normal(keys[1], shape), -4.0, 4.0)
    tone_amp = jax.random.uniform(keys[2], small, minval=0.0, maxval=3.0)
    offsets = jax.random.uniform(keys[3], small, minval=-2.0, maxval=2.0)
    tone_bins = jax.random.randint(keys[4], small, F0, F0 + NF)
    tone_phase = jax.random.uniform(keys[5], small, minval=-math.pi, maxval=math.pi)
    sample_ids = jnp.arange(SAMP, dtype=jnp.int32)
    cycles = tone_bins * sample_ids[None, None, :] % SAMP
    tone = tone_amp * jnp.cos(cycles.astype(jnp.float32) * (2.0 * math.pi / SAMP) + tone_phase)
    return scales * (noise + tone) + offsets


def draw_live_counts(key, part):
    key = jax.random.fold_in(key, 23)
    keys = jax.random.split(key, 2)
    counts = jax.random.randint(keys[0], (N_CHAN,), 1, CH + 1)
    fullest = jax.random.randint(keys[1], (), 0, N_CHAN)
    return jnp.where(jnp.arange(N_CHAN) == fullest, CH, counts).astype(jnp.int32)


def draw_pair_lists(key, part):
    key = jax.random.fold_in(key, 37)
    keys = jax.random.split(key, 4)
    used = jax.random.randint(keys[0], (N_CHAN,), 1, PMAX + 1)
    fullest = jax.random.randint(keys[1], (), 0, N_CHAN)
    used = jnp.where(jnp.arange(N_CHAN) == fullest, PMAX, used)
    first = jax.random.randint(keys[2], (N_CHAN, PMAX), 0, N_CHAN)
    second = jax.random.randint(keys[3], (N_CHAN, PMAX), 0, N_CHAN)
    lower = jnp.minimum(first, second)
    upper = jnp.maximum(first, second)
    valid_flag = (jnp.arange(PMAX)[None, :] < used[:, None]).astype(jnp.int32)
    return jnp.stack([lower * valid_flag, upper * valid_flag, valid_flag], axis=-1).astype(jnp.int32)


def setup_inputs(seed: int = 0) -> dict:
    key_list = jax.random.split(jax.random.key(seed), 4)
    return {
        "traces": draw_traces(jax.random.fold_in(key_list[3], 71), 0),
        "live_counts": draw_live_counts(jax.random.fold_in(key_list[3], 71), 0),
        "pair_lists": draw_pair_lists(jax.random.fold_in(key_list[3], 71), 0),
    }


def band_tables():
    sample_ids = jnp.arange(SAMP, dtype=jnp.int32)
    bins = F0 + jnp.arange(NF, dtype=jnp.int32)
    phases = sample_ids[:, None] * bins[None, :] % SAMP
    angles = phases.astype(jnp.float32) * (2.0 * math.pi / SAMP)
    forward = jnp.concatenate([jnp.cos(angles), -jnp.sin(angles)], axis=1)
    lag_ids = jnp.arange(NLAG, dtype=jnp.int32) - NLAG // 2
    lag_phases = bins[:, None] * lag_ids[None, :] % SAMP
    lag_angles = lag_phases.astype(jnp.float32) * (2.0 * math.pi / SAMP)
    inverse = jnp.concatenate([jnp.cos(lag_angles), -jnp.sin(lag_angles)], axis=0)
    taper = 0.5 - 0.5 * jnp.cos(sample_ids.astype(jnp.float32) * (2.0 * math.pi / SAMP))
    return (forward, inverse, taper)

def whiten(traces, live, forward, taper):
    channel_total, window_total, samples = traces.shape
    centred = traces - lax.optimization_barrier(jnp.mean(traces, axis=2, keepdims=True))
    tapered = (centred * taper).reshape(-1, samples)
    spectra = jnp.dot(tapered, forward, precision=lax.Precision.HIGHEST, preferred_element_type=jnp.float32)
    power = lax.optimization_barrier(jnp.sum(spectra * spectra, axis=1, keepdims=True)) / NF
    white = spectra / jnp.sqrt(power + 1e-06)
    return white.reshape(channel_total, window_total, 2 * NF) * live[:, None, None]

def cross_spectrum(first_block, second_block):
    real_a, imag_a = (first_block[..., :NF], first_block[..., NF:])
    real_b, imag_b = (second_block[..., :NF], second_block[..., NF:])
    high = lax.Precision.HIGHEST
    real_part = jnp.einsum('awk,bwk->abk', real_a, real_b, precision=high) + jnp.einsum('awk,bwk->abk', imag_a, imag_b, precision=high)
    imag_part = jnp.einsum('awk,bwk->abk', imag_a, real_b, precision=high) - jnp.einsum('awk,bwk->abk', real_a, imag_b, precision=high)
    return jnp.concatenate([real_part, imag_part], axis=-1).reshape(CH * CH, 2 * NF)

def reference(traces, live_counts, pair_lists):
    forward, inverse, taper = band_tables()
    channel_ids = jnp.arange(CHANNELS, dtype=jnp.int32)
    live = (channel_ids % CH < live_counts[channel_ids // CH]).astype(jnp.float32)
    white = whiten(traces, live, forward, taper)
    blocks = white.reshape(N_CHAN, CH, WINDOWS, 2 * NF)
    slot_lists = pair_lists.reshape(N_CHAN * PMAX, 3)
    scaling = 1.0 / math.sqrt(WINDOWS * NF)

    def one_slot(entry):
        spectrum = cross_spectrum(blocks[entry[0]], blocks[entry[1]]) * entry[2].astype(jnp.float32)
        return jnp.dot(spectrum, inverse, precision=lax.Precision.HIGHEST, preferred_element_type=jnp.float32) * scaling
    stacks = lax.map(one_slot, slot_lists)
    return jnp.transpose(stacks, (1, 0, 2))
```

```python
import functools
import math

import jax
import jax.numpy as jnp
import ml_dtypes
import numpy as np
from jax import lax
from jax.experimental import pallas as pl
from jax.experimental.pallas import tpu as pltpu
from jax.sharding import PartitionSpec as P

SAMP = 1024
F0 = 2
NF = 128
NLAG = 256
LANES = 128
MESH = pl.DeviceIdType.MESH


def split_table(table):
    high = table.astype(np.float32).astype(ml_dtypes.bfloat16)
    low = (table - high.astype(np.float64)).astype(np.float32).astype(ml_dtypes.bfloat16)
    return high, low


@functools.lru_cache
def forward_tables():
    samples = np.arange(SAMP)
    bins = F0 + np.arange(NF)
    angles = (samples[:, None] * bins[None, :] % SAMP) * (2.0 * math.pi / SAMP)
    taper = 0.5 - 0.5 * np.cos(samples * (2.0 * math.pi / SAMP))
    return split_table(taper[:, None] * np.concatenate([np.cos(angles), -np.sin(angles)], axis=1))


@functools.lru_cache
def inverse_tables(window_total):
    bins = F0 + np.arange(NF)
    lags = np.arange(NLAG) - NLAG // 2
    angles = (bins[:, None] * lags[None, :] % SAMP) * (2.0 * math.pi / SAMP)
    table = np.concatenate([np.cos(angles), -np.sin(angles)], axis=0)
    return split_table(table / math.sqrt(window_total * NF))


def split(value):
    high = value.astype(jnp.bfloat16)
    return high, (value - high.astype(jnp.float32)).astype(jnp.bfloat16)


def dot(left, right):
    return jnp.dot(left, right, preferred_element_type=jnp.float32)


def whitened(block, windows, count_ref, traces_ref, high_ref, low_ref):
    tiles = SAMP // LANES
    parts = []
    for w in range(windows):
        pieces = [
            traces_ref[pl.ds(tile * windows + w, block, stride=tiles * windows), :]
            for tile in range(tiles)
        ]
        parts.append(jnp.concatenate(pieces, axis=1))
    samples = jnp.concatenate(parts, axis=0)
    centred = samples - jnp.sum(samples, axis=1, keepdims=True) * (1.0 / SAMP)
    high, low = split(centred)
    spectra = dot(high, high_ref[...]) + dot(low, high_ref[...]) + dot(high, low_ref[...])
    power = jnp.sum(spectra * spectra, axis=1, keepdims=True) * (1.0 / NF)
    channel = lax.broadcasted_iota(jnp.int32, (windows * block, 1), 0) % block
    live = (channel < count_ref[0]).astype(jnp.float32)
    return spectra * (live / jnp.sqrt(power + 1e-06))


def white_kernel(block, windows, count_ref, traces_ref, high_ref, low_ref, out_ref):
    out_ref[...] = whitened(block, windows, count_ref, traces_ref, high_ref, low_ref)


def gather_kernel(
    block, windows, z_total, count_ref, traces_ref, high_ref, low_ref, held,
    z_send, z_recv, x_send, x_recv, y_send, y_recv, f_send, f_recv, s_send, s_recv,
):
    me = lax.axis_index("chan")
    y = lax.axis_index("win")
    z, x, core = me // 4, (me // 2) % 2, me % 2

    def chan_of(z_at, x_at, core_at):
        return z_at * 4 + x_at * 2 + core_at

    along_z = [((z + d) % z_total) for d in range(z_total)]
    x_peer = (chan_of(z, 1 - x, core), y)
    y_peer = (me, 1 - y)
    sibling = (chan_of(z, x, 1 - core), y)
    barrier = pltpu.get_barrier_semaphore()
    peers = [(chan_of(along_z[d], x, core), y) for d in range(1, z_total)]
    peers += [x_peer, y_peer, sibling]
    for peer in peers:
        pl.semaphore_signal(barrier, inc=1, device_id=peer, device_id_type=MESH)

    held[y, me] = whitened(block, windows, count_ref, traces_ref, high_ref, low_ref)
    pl.semaphore_wait(barrier, len(peers))

    sent = []
    incoming = {}

    def send(y_at, chan_at, send_sem, recv_sem, peer):
        copy = pltpu.make_async_remote_copy(
            src_ref=held.at[y_at, chan_at],
            dst_ref=held.at[y_at, chan_at],
            send_sem=send_sem,
            recv_sem=recv_sem,
            device_id=peer,
            device_id_type=MESH,
        )
        copy.start()
        sent.append(copy)
        return copy

    def to_sibling(slot, y_at, chan_at):
        send(y_at, chan_at, s_send.at[slot], s_recv.at[slot], sibling)

    send(y, me, x_send.at[0], x_recv.at[0], x_peer)
    send(y, me, y_send.at[0], y_recv.at[0], y_peer)
    z_copies = [None]
    for d in range(1, z_total):
        to_z = (z + z_total - d) % z_total
        z_copies.append(send(y, me, z_send.at[d], z_recv.at[d], (chan_of(to_z, x, core), y)))
    to_sibling(0, y, me)

    def wait_arrival(recv_sem):
        pltpu.make_async_copy(held.at[y, me], held.at[y, me], recv_sem).wait()

    for d in range(z_total):
        column = chan_of(along_z[d], x, core)
        across = chan_of(along_z[d], 1 - x, core)
        if d > 0:
            z_copies[d].wait_recv()
            send(y, column, x_send.at[d], x_recv.at[d], x_peer)
            send(y, column, y_send.at[d], y_recv.at[d], y_peer)
            to_sibling(4 * d, y, column)
        wait_arrival(x_recv.at[d])
        if d % 2 == 0:
            send(y, across, f_send.at[d], f_recv.at[d], y_peer)
        to_sibling(4 * d + 1, y, across)
        wait_arrival(y_recv.at[d])
        if d % 2 == 1:
            send(1 - y, column, f_send.at[d], f_recv.at[d], x_peer)
        to_sibling(4 * d + 2, 1 - y, column)
    for d in range(z_total):
        wait_arrival(f_recv.at[d])
        to_sibling(4 * d + 3, 1 - y, chan_of(along_z[d], 1 - x, core))
    for slot in range(4 * z_total):
        wait_arrival(s_recv.at[slot])
    for copy in sent:
        copy.wait_send()


def lag_kernel(block, chunk, slots, pairs_ref, place_ref, *refs):
    firsts, seconds = refs[:slots], refs[slots : 2 * slots]
    high_table, low_table, out_ref, high_ref, low_ref = refs[2 * slots :]
    rows = chunk * block
    y_total, _, local = firsts[0].shape[:3]
    windows = [(yy, ww) for yy in range(y_total) for ww in range(local // block)]
    start = place_ref[0] + pl.program_id(0) * chunk
    for p in range(slots):
        valid = pairs_ref[3 * p + 2].astype(jnp.float32)
        for i in range(chunk):
            real = jnp.zeros((block, NF), jnp.float32)
            imag = jnp.zeros((block, NF), jnp.float32)
            for yy, ww in windows:
                a = firsts[p][yy, 0, pl.ds(ww * block + start + i, 1), :] * valid
                real_a, imag_a = a[:, :NF], a[:, NF:]
                real_b = seconds[p][yy, 0, ww * block : (ww + 1) * block, :NF]
                imag_b = seconds[p][yy, 0, ww * block : (ww + 1) * block, NF:]
                real = real + (real_a * real_b + imag_a * imag_b)
                imag = imag + (imag_a * real_b - real_a * imag_b)
            at = pl.ds(p * rows + i * block, block)
            high_ref[at, :NF], low_ref[at, :NF] = split(real)
            high_ref[at, NF:], low_ref[at, NF:] = split(imag)
    for p in range(slots):
        at = pl.ds(p * rows, rows)
        high, low = high_ref[at, :], low_ref[at, :]
        lagged = dot(high, high_table[...]) + dot(low, high_table[...]) + dot(high, low_table[...])
        for h in range(NLAG // LANES):
            out_ref[pl.ds(h * slots + p, rows, stride=slots * (NLAG // LANES)), :] = lagged[
                :, h * LANES : (h + 1) * LANES
            ]


def body(routed, chan_total, win_total, traces, live_counts, pair_lists):
    block, windows, samples = traces.shape
    slots = pair_lists.shape[1]
    high, low = (jnp.asarray(t) for t in forward_tables())
    tiles = samples // LANES
    linear = traces.reshape(block, windows, tiles, LANES).transpose(0, 2, 1, 3)
    linear = linear.reshape(block * tiles * windows, LANES)
    vmem = pl.BlockSpec(memory_space=pltpu.VMEM)
    smem = pl.BlockSpec(memory_space=pltpu.SMEM)
    local = windows * block
    if routed:
        z_total = chan_total // 4
        dma = pltpu.SemaphoreType.DMA
        held = pl.pallas_call(
            functools.partial(gather_kernel, block, windows, z_total),
            out_shape=jax.ShapeDtypeStruct((win_total, chan_total, local, 2 * NF), jnp.float32),
            in_specs=[smem, vmem, vmem, vmem],
            out_specs=vmem,
            scratch_shapes=[dma((z_total,))] * 8 + [dma((4 * z_total,))] * 2,
            compiler_params=pltpu.CompilerParams(
                collective_id=0, has_side_effects=True, vmem_limit_bytes=24 * 2**20
            ),
            name="whiten_gather",
        )(live_counts, linear, high, low)
    else:
        white = pl.pallas_call(
            functools.partial(white_kernel, block, windows),
            out_shape=jax.ShapeDtypeStruct((local, 2 * NF), jnp.float32),
            in_specs=[smem, vmem, vmem, vmem],
            out_specs=vmem,
            compiler_params=pltpu.CompilerParams(vmem_limit_bytes=24 * 2**20),
            name="whiten",
        )(live_counts, linear, high, low)
        held = lax.all_gather(white, ("win", "chan"), axis=0, tiled=False)
        held = held.reshape(win_total, chan_total, local, 2 * NF)

    firsts = block // win_total
    chunk = min(4, firsts)
    rows = chunk * block
    inv_high, inv_low = (jnp.asarray(t) for t in inverse_tables(windows * win_total))
    place = (lax.axis_index("win") * firsts).astype(jnp.int32).reshape(1)
    pairs = pair_lists.reshape(slots * 3)
    spec = (win_total, 1, local, 2 * NF)

    def block_spec(entry):
        return pl.BlockSpec(spec, lambda g, pairs, place: (0, pairs[entry], 0, 0))

    table_spec = pl.BlockSpec((2 * NF, NLAG), lambda g, pairs, place: (0, 0))
    tall = slots * (NLAG // LANES)
    out = pl.pallas_call(
        functools.partial(lag_kernel, block, chunk, slots),
        out_shape=jax.ShapeDtypeStruct((firsts * block * tall, LANES), jnp.float32),
        grid_spec=pltpu.PrefetchScalarGridSpec(
            num_scalar_prefetch=2,
            grid=(firsts // chunk,),
            in_specs=[block_spec(3 * p) for p in range(slots)]
            + [block_spec(3 * p + 1) for p in range(slots)]
            + [table_spec, table_spec],
            out_specs=pl.BlockSpec((rows * tall, LANES), lambda g, pairs, place: (g, 0)),
            scratch_shapes=[pltpu.VMEM((slots * rows, 2 * NF), jnp.bfloat16)] * 2,
        ),
        compiler_params=pltpu.CompilerParams(vmem_limit_bytes=32 * 2**20),
        name="cross_lags",
    )(pairs, place, *([held] * (2 * slots)), inv_high, inv_low)
    out = out.reshape(firsts * block, NLAG // LANES, slots, LANES).transpose(0, 2, 1, 3)
    return out.reshape(firsts * block, slots, NLAG)


def solution(mesh):
    chan_total, win_total = mesh.shape["chan"], mesh.shape["win"]
    routed = (chan_total, win_total) == (16, 2)
    return jax.shard_map(
        functools.partial(body, routed, chan_total, win_total),
        mesh=mesh,
        in_specs=(P("chan", "win", None), P("chan"), P("chan", None, None)),
        out_specs=P("win", "chan", None),
        check_vma=False,
    )
```

```python
import functools
import math

import jax
import jax.numpy as jnp
import ml_dtypes
import numpy as np
from jax import lax
from jax.experimental import pallas as pl
from jax.experimental.pallas import tpu as pltpu
from jax.sharding import PartitionSpec as P

SAMP = 1024
F0 = 2
NF = 128
NLAG = 256
LANES = 128
MESH = pl.DeviceIdType.MESH


def split_table(table):
    high = table.astype(np.float32).astype(ml_dtypes.bfloat16)
    low = (table - high.astype(np.float64)).astype(np.float32).astype(ml_dtypes.bfloat16)
    return high, low


@functools.lru_cache
def forward_tables():
    samples = np.arange(SAMP)
    bins = F0 + np.arange(NF)
    angles = (samples[:, None] * bins[None, :] % SAMP) * (2.0 * math.pi / SAMP)
    taper = 0.5 - 0.5 * np.cos(samples * (2.0 * math.pi / SAMP))
    return split_table(taper[:, None] * np.concatenate([np.cos(angles), -np.sin(angles)], axis=1))


@functools.lru_cache
def inverse_tables(window_total):
    bins = F0 + np.arange(NF)
    lags = np.arange(NLAG) - NLAG // 2
    angles = (bins[:, None] * lags[None, :] % SAMP) * (2.0 * math.pi / SAMP)
    table = np.concatenate([np.cos(angles), -np.sin(angles)], axis=0)
    return split_table(table / math.sqrt(window_total * NF))


def split(value):
    high = value.astype(jnp.bfloat16)
    return high, (value - high.astype(jnp.float32)).astype(jnp.bfloat16)


def dot(left, right):
    return jnp.dot(left, right, preferred_element_type=jnp.float32)


def whitened(block, windows, count_ref, traces_ref, high_ref, low_ref):
    tiles = SAMP // LANES
    parts = []
    for w in range(windows):
        pieces = [
            traces_ref[pl.ds(tile * windows + w, block, stride=tiles * windows), :]
            for tile in range(tiles)
        ]
        parts.append(jnp.concatenate(pieces, axis=1))
    samples = jnp.concatenate(parts, axis=0)
    centred = samples - jnp.sum(samples, axis=1, keepdims=True) * (1.0 / SAMP)
    high, low = split(centred)
    spectra = dot(high, high_ref[...]) + dot(low, high_ref[...]) + dot(high, low_ref[...])
    power = jnp.sum(spectra * spectra, axis=1, keepdims=True) * (1.0 / NF)
    channel = lax.broadcasted_iota(jnp.int32, (windows * block, 1), 0) % block
    live = (channel < count_ref[0]).astype(jnp.float32)
    return spectra * (live / jnp.sqrt(power + 1e-06))


def white_kernel(block, windows, count_ref, traces_ref, high_ref, low_ref, out_ref):
    out_ref[...] = whitened(block, windows, count_ref, traces_ref, high_ref, low_ref)


def gather_kernel(
    block, windows, count_ref, traces_hbm, high_hbm, low_hbm, held, traces_ref, high_ref, low_ref,
    load, send_sem, link_recv, core_recv,
):
    loads = [
        pltpu.make_async_copy(source, target, load.at[i])
        for i, (source, target) in enumerate(
            [(traces_hbm, traces_ref), (high_hbm, high_ref), (low_hbm, low_ref)]
        )
    ]
    for copy in loads:
        copy.start()
    me = lax.axis_index("chan")
    y = lax.axis_index("win")
    z, x, core = me // 4, (me // 2) % 2, me % 2

    def chan_of(z_at, x_at, core_at):
        return z_at * 4 + x_at * 2 + core_at

    upper = z // 2
    pair = z + 1 - 2 * (z % 2)
    near, far = 2 - upper, 3 - 3 * upper
    x_peer = (chan_of(z, 1 - x, core), y)
    y_peer = (me, 1 - y)
    diagonal = (chan_of(z, 1 - x, core), 1 - y)
    sibling = (chan_of(z, x, 1 - core), y)
    pair_peer, near_peer, far_peer = ((chan_of(at, x, core), y) for at in (pair, near, far))
    barrier = pltpu.get_barrier_semaphore()
    peers = (x_peer, y_peer, diagonal, sibling, pair_peer, near_peer, far_peer)
    for peer in peers:
        pl.semaphore_signal(barrier, inc=1, device_id=peer, device_id_type=MESH)
    for copy in loads:
        copy.wait()
    held[y, me] = whitened(block, windows, count_ref, traces_ref, high_ref, low_ref)
    pl.semaphore_wait(barrier, len(peers))

    sent = []

    def shard(z_at, kind, core_at):
        x_at = x if kind % 2 == 0 else 1 - x
        y_at = y if kind < 2 else 1 - y
        return held.at[y_at, chan_of(z_at, x_at, core_at)]

    def send(part, recv_sem, peer):
        copy = pltpu.make_async_remote_copy(
            src_ref=part,
            dst_ref=part,
            send_sem=send_sem.at[len(sent)],
            recv_sem=recv_sem,
            device_id=peer,
            device_id_type=MESH,
        )
        copy.start()
        sent.append(copy)

    def to_link(z_at, kind, kind_there, peer):
        send(shard(z_at, kind, core), link_recv.at[4 * z_at + kind_there], peer)

    def to_core(z_at, kind):
        send(shard(z_at, kind, core), core_recv.at[4 * z_at + kind], sibling)

    def arrived(z_at, kind):
        part = shard(z_at, kind, core)
        pltpu.make_async_copy(part, part, link_recv.at[4 * z_at + kind]).wait()

    to_link(z, 0, 0, near_peer)
    to_link(z, 0, 1, x_peer)
    to_link(z, 0, 2, y_peer)
    to_link(z, 0, 0, far_peer)
    to_link(z, 0, 3, diagonal)
    to_link(z, 0, 0, pair_peer)
    to_core(z, 0)

    def hand_to_pair(kind):
        arrived(z, kind)
        to_link(z, kind, kind, pair_peer)
        to_core(z, kind)

    def spread(z_at):
        arrived(z_at, 0)
        to_link(z_at, 0, 1, x_peer)
        to_link(z_at, 0, 2, y_peer)
        to_link(z_at, 0, 3, diagonal)
        to_core(z_at, 0)

    def hand_on(z_at, kind):
        arrived(z_at, kind)
        to_core(z_at, kind)

    hand_to_pair(1)
    hand_to_pair(2)
    spread(near)
    hand_to_pair(3)
    spread(far)
    for kind in range(4):
        hand_on(pair, kind)
    for z_at in (near, far):
        for kind in range(1, 4):
            hand_on(z_at, kind)
    for z_at in range(4):
        for kind in range(4):
            part = shard(z_at, kind, 1 - core)
            pltpu.make_async_copy(part, part, core_recv.at[4 * z_at + kind]).wait()
    for copy in sent:
        copy.wait_send()


def lag_kernel(block, chunk, slots, pairs_ref, place_ref, *refs):
    firsts, seconds = refs[:slots], refs[slots : 2 * slots]
    high_table, low_table, out_ref, high_ref, low_ref = refs[2 * slots :]
    rows = chunk * block
    y_total, _, local = firsts[0].shape[:3]
    windows = [(yy, ww) for yy in range(y_total) for ww in range(local // block)]
    start = place_ref[0] + pl.program_id(0) * chunk
    for p in range(slots):
        valid = pairs_ref[2, 0, p].astype(jnp.float32)
        for i in range(chunk):
            real = jnp.zeros((block, NF), jnp.float32)
            imag = jnp.zeros((block, NF), jnp.float32)
            for yy, ww in windows:
                a = firsts[p][yy, 0, pl.ds(ww * block + start + i, 1), :] * valid
                real_a, imag_a = a[:, :NF], a[:, NF:]
                real_b = seconds[p][yy, 0, ww * block : (ww + 1) * block, :NF]
                imag_b = seconds[p][yy, 0, ww * block : (ww + 1) * block, NF:]
                real = real + (real_a * real_b + imag_a * imag_b)
                imag = imag + (imag_a * real_b - real_a * imag_b)
            at = pl.ds(p * rows + i * block, block)
            high_ref[at, :NF], low_ref[at, :NF] = split(real)
            high_ref[at, NF:], low_ref[at, NF:] = split(imag)
    for p in range(slots):
        at = pl.ds(p * rows, rows)
        high, low = high_ref[at, :], low_ref[at, :]
        lagged = dot(high, high_table[...]) + dot(low, high_table[...]) + dot(high, low_table[...])
        for h in range(NLAG // LANES):
            out_ref[pl.ds(h * slots + p, rows, stride=slots * (NLAG // LANES)), :] = lagged[
                :, h * LANES : (h + 1) * LANES
            ]


def body(routed, chan_total, win_total, traces, live_counts, pair_lists):
    block, windows, samples = traces.shape
    slots = pair_lists.shape[1]
    high, low = (jnp.asarray(t) for t in forward_tables())
    tiles = samples // LANES
    linear = traces.reshape(block, windows, tiles, LANES).transpose(0, 2, 1, 3)
    linear = linear.reshape(block * tiles * windows, LANES)
    vmem = pl.BlockSpec(memory_space=pltpu.VMEM)
    smem = pl.BlockSpec(memory_space=pltpu.SMEM)
    local = windows * block
    if routed:
        dma = pltpu.SemaphoreType.DMA
        hbm = pl.BlockSpec(memory_space=pltpu.MemorySpace.HBM)

        def in_hbm(value):
            return pltpu.with_memory_space_constraint(value, pltpu.MemorySpace.HBM)

        held = pl.pallas_call(
            functools.partial(gather_kernel, block, windows),
            out_shape=jax.ShapeDtypeStruct((win_total, chan_total, local, 2 * NF), jnp.float32),
            in_specs=[smem, hbm, hbm, hbm],
            out_specs=vmem,
            scratch_shapes=[
                pltpu.VMEM(linear.shape, linear.dtype),
                pltpu.VMEM(high.shape, high.dtype),
                pltpu.VMEM(low.shape, low.dtype),
                dma((3,)),
                dma((31,)),
                dma((16,)),
                dma((16,)),
            ],
            compiler_params=pltpu.CompilerParams(
                collective_id=0, has_side_effects=True, vmem_limit_bytes=24 * 2**20
            ),
            name="whiten_gather",
        )(live_counts, *(in_hbm(value) for value in (linear, high, low)))
    else:
        white = pl.pallas_call(
            functools.partial(white_kernel, block, windows),
            out_shape=jax.ShapeDtypeStruct((local, 2 * NF), jnp.float32),
            in_specs=[smem, vmem, vmem, vmem],
            out_specs=vmem,
            compiler_params=pltpu.CompilerParams(vmem_limit_bytes=24 * 2**20),
            name="whiten",
        )(live_counts, linear, high, low)
        held = lax.all_gather(white, ("win", "chan"), axis=0, tiled=False)
        held = held.reshape(win_total, chan_total, local, 2 * NF)

    firsts = block // win_total
    chunk = min(4, firsts)
    rows = chunk * block
    inv_high, inv_low = (jnp.asarray(t) for t in inverse_tables(windows * win_total))
    place = (lax.axis_index("win") * firsts).astype(jnp.int32).reshape(1)
    pairs = pair_lists.transpose(2, 0, 1)
    spec = (win_total, 1, local, 2 * NF)

    def block_spec(entry, p):
        return pl.BlockSpec(spec, lambda g, pairs, place: (0, pairs[entry, 0, p], 0, 0))

    table_spec = pl.BlockSpec((2 * NF, NLAG), lambda g, pairs, place: (0, 0))
    tall = slots * (NLAG // LANES)
    out = pl.pallas_call(
        functools.partial(lag_kernel, block, chunk, slots),
        out_shape=jax.ShapeDtypeStruct((firsts * block * tall, LANES), jnp.float32),
        grid_spec=pltpu.PrefetchScalarGridSpec(
            num_scalar_prefetch=2,
            grid=(firsts // chunk,),
            in_specs=[block_spec(0, p) for p in range(slots)]
            + [block_spec(1, p) for p in range(slots)]
            + [table_spec, table_spec],
            out_specs=pl.BlockSpec((rows * tall, LANES), lambda g, pairs, place: (g, 0)),
            scratch_shapes=[pltpu.VMEM((slots * rows, 2 * NF), jnp.bfloat16)] * 2,
        ),
        compiler_params=pltpu.CompilerParams(vmem_limit_bytes=32 * 2**20),
        name="cross_lags",
    )(pairs, place, *([held] * (2 * slots)), inv_high, inv_low)
    out = out.reshape(firsts * block, NLAG // LANES, slots, LANES).transpose(0, 2, 1, 3)
    return out.reshape(firsts * block, slots, NLAG)


def solution(mesh):
    chan_total, win_total = mesh.shape["chan"], mesh.shape["win"]
    routed = (chan_total, win_total) == (16, 2)
    return jax.shard_map(
        functools.partial(body, routed, chan_total, win_total),
        mesh=mesh,
        in_specs=(P("chan", "win", None), P("chan"), P("chan", None, None)),
        out_specs=P("win", "chan", None),
        check_vma=False,
    )
```

```python
import functools
import math

import jax
import jax.numpy as jnp
import ml_dtypes
import numpy as np
from jax import lax
from jax.experimental import pallas as pl
from jax.experimental.pallas import tpu as pltpu
from jax.sharding import PartitionSpec as P

SAMP = 1024
F0 = 2
NF = 128
NLAG = 256
LANES = 128
MESH = pl.DeviceIdType.MESH


def split_table(table):
    high = table.astype(np.float32).astype(ml_dtypes.bfloat16)
    low = (table - high.astype(np.float64)).astype(np.float32).astype(ml_dtypes.bfloat16)
    return high, low


@functools.lru_cache
def forward_tables():
    samples = np.arange(SAMP)
    bins = F0 + np.arange(NF)
    angles = (samples[:, None] * bins[None, :] % SAMP) * (2.0 * math.pi / SAMP)
    taper = 0.5 - 0.5 * np.cos(samples * (2.0 * math.pi / SAMP))
    return split_table(taper[:, None] * np.concatenate([np.cos(angles), -np.sin(angles)], axis=1))


@functools.lru_cache
def inverse_tables(window_total):
    bins = F0 + np.arange(NF)
    lags = np.arange(NLAG) - NLAG // 2
    angles = (bins[:, None] * lags[None, :] % SAMP) * (2.0 * math.pi / SAMP)
    table = np.concatenate([np.cos(angles), -np.sin(angles)], axis=0)
    return split_table(table / math.sqrt(window_total * NF))


def split(value):
    high = value.astype(jnp.bfloat16)
    return high, (value - high.astype(jnp.float32)).astype(jnp.bfloat16)


def dot(left, right):
    return jnp.dot(left, right, preferred_element_type=jnp.float32)


def whitened(block, windows, count_ref, traces_ref, high_ref, low_ref):
    tiles = SAMP // LANES
    parts = []
    for w in range(windows):
        pieces = [
            traces_ref[pl.ds(tile * windows + w, block, stride=tiles * windows), :]
            for tile in range(tiles)
        ]
        parts.append(jnp.concatenate(pieces, axis=1))
    samples = jnp.concatenate(parts, axis=0)
    centred = samples - jnp.sum(samples, axis=1, keepdims=True) * (1.0 / SAMP)
    high, low = split(centred)
    spectra = dot(high, high_ref[...]) + dot(low, high_ref[...]) + dot(high, low_ref[...])
    power = jnp.sum(spectra * spectra, axis=1, keepdims=True) * (1.0 / NF)
    channel = lax.broadcasted_iota(jnp.int32, (windows * block, 1), 0) % block
    live = (channel < count_ref[0]).astype(jnp.float32)
    return spectra * (live / jnp.sqrt(power + 1e-06))


def white_kernel(block, windows, count_ref, traces_ref, high_ref, low_ref, out_ref):
    out_ref[...] = whitened(block, windows, count_ref, traces_ref, high_ref, low_ref)


def gather_kernel(
    block, windows, count_ref, traces_hbm, high_hbm, low_hbm, held, traces_ref, high_ref, low_ref,
    load, send_sem, link_recv, core_recv,
):
    loads = [
        pltpu.make_async_copy(source, target, load.at[i])
        for i, (source, target) in enumerate(
            [(traces_hbm, traces_ref), (high_hbm, high_ref), (low_hbm, low_ref)]
        )
    ]
    for copy in loads:
        copy.start()
    me = lax.axis_index("chan")
    y = lax.axis_index("win")
    z, x, core = me // 4, (me // 2) % 2, me % 2

    def chan_of(z_at, x_at, core_at):
        return z_at * 4 + x_at * 2 + core_at

    upper = z // 2
    pair = z + 1 - 2 * (z % 2)
    near, far = 2 - upper, 3 - 3 * upper
    x_peer = (chan_of(z, 1 - x, core), y)
    y_peer = (me, 1 - y)
    diagonal = (chan_of(z, 1 - x, core), 1 - y)
    sibling = (chan_of(z, x, 1 - core), y)
    pair_peer, near_peer, far_peer = ((chan_of(at, x, core), y) for at in (pair, near, far))
    barrier = pltpu.get_barrier_semaphore()
    peers = (x_peer, y_peer, diagonal, sibling, pair_peer, near_peer, far_peer)
    for peer in peers:
        pl.semaphore_signal(barrier, inc=1, device_id=peer, device_id_type=MESH)
    for copy in loads:
        copy.wait()
    held[y, me] = whitened(block, windows, count_ref, traces_ref, high_ref, low_ref)
    pl.semaphore_wait(barrier, len(peers))

    sent = []

    def shard(z_at, kind, core_at):
        x_at = x if kind % 2 == 0 else 1 - x
        y_at = y if kind < 2 else 1 - y
        return held.at[y_at, chan_of(z_at, x_at, core_at)]

    def send(part, recv_sem, peer):
        copy = pltpu.make_async_remote_copy(
            src_ref=part,
            dst_ref=part,
            send_sem=send_sem.at[len(sent)],
            recv_sem=recv_sem,
            device_id=peer,
            device_id_type=MESH,
        )
        copy.start()
        sent.append(copy)

    def to_link(z_at, kind, kind_there, peer):
        send(shard(z_at, kind, core), link_recv.at[4 * z_at + kind_there], peer)

    def to_core(z_at, kind):
        send(shard(z_at, kind, core), core_recv.at[4 * z_at + kind], sibling)

    def arrived(z_at, kind):
        part = shard(z_at, kind, core)
        pltpu.make_async_copy(part, part, link_recv.at[4 * z_at + kind]).wait()

    to_link(z, 0, 0, near_peer)
    to_link(z, 0, 1, x_peer)
    to_link(z, 0, 2, y_peer)
    to_link(z, 0, 0, far_peer)
    to_link(z, 0, 3, diagonal)
    to_link(z, 0, 0, pair_peer)
    to_core(z, 0)

    def hand_to_pair(kind):
        arrived(z, kind)
        to_link(z, kind, kind, pair_peer)
        to_core(z, kind)

    def spread(z_at):
        arrived(z_at, 0)
        to_link(z_at, 0, 1, x_peer)
        to_link(z_at, 0, 2, y_peer)
        to_link(z_at, 0, 3, diagonal)
        to_core(z_at, 0)

    def hand_on(z_at, kind):
        arrived(z_at, kind)
        to_core(z_at, kind)

    hand_to_pair(1)
    hand_to_pair(2)
    spread(near)
    hand_to_pair(3)
    spread(far)
    for kind in range(4):
        hand_on(pair, kind)
    for z_at in (near, far):
        for kind in range(1, 4):
            hand_on(z_at, kind)
    for z_at in range(4):
        for kind in range(4):
            part = shard(z_at, kind, 1 - core)
            pltpu.make_async_copy(part, part, core_recv.at[4 * z_at + kind]).wait()
    for copy in sent:
        copy.wait_send()


def lag_kernel(
    block, chunk, slots, pairs_ref, place_ref, held_ref, high_table, low_table, out_hbm,
    high_ref, low_ref, out_ref, stored,
):
    rows = chunk * block
    tall = slots * (NLAG // LANES)
    y_total, _, local = held_ref.shape[:3]
    windows = [(yy, ww) for yy in range(y_total) for ww in range(local // block)]
    groups = out_ref.shape[0]

    def store(group):
        return pltpu.make_async_copy(
            out_ref.at[group],
            out_hbm.at[pl.ds(group * (rows * tall), rows * tall)],
            stored.at[group],
        )

    def make_group(group, carry):
        start = place_ref[0] + group * chunk
        for p in range(slots):
            first, second = pairs_ref[0, 0, p], pairs_ref[1, 0, p]
            valid = pairs_ref[2, 0, p].astype(jnp.float32)
            for i in range(0, chunk, 2):
                real = [jnp.zeros((block, NF), jnp.float32)] * 2
                imag = [jnp.zeros((block, NF), jnp.float32)] * 2
                for yy, ww in windows:
                    real_b = held_ref[yy, second, ww * block : (ww + 1) * block, :NF]
                    imag_b = held_ref[yy, second, ww * block : (ww + 1) * block, NF:]
                    for j in range(2):
                        a = held_ref[yy, first, pl.ds(ww * block + start + i + j, 1), :] * valid
                        real_a, imag_a = a[:, :NF], a[:, NF:]
                        real[j] = real[j] + (real_a * real_b + imag_a * imag_b)
                        imag[j] = imag[j] + (imag_a * real_b - real_a * imag_b)
                for j in range(2):
                    at = pl.ds(p * rows + (i + j) * block, block)
                    high_ref[at, :NF], low_ref[at, :NF] = split(real[j])
                    high_ref[at, NF:], low_ref[at, NF:] = split(imag[j])
            at = pl.ds(p * rows, rows)
            high, low = high_ref[at, :], low_ref[at, :]
            lagged = (
                dot(high, high_table[...]) + dot(low, high_table[...]) + dot(high, low_table[...])
            )
            for h in range(NLAG // LANES):
                out_ref[group, pl.ds(h * slots + p, rows, stride=tall), :] = lagged[
                    :, h * LANES : (h + 1) * LANES
                ]
        store(group).start()
        return carry

    lax.fori_loop(0, groups, make_group, 0)
    for group in range(groups):
        store(group).wait()


def body(routed, chan_total, win_total, traces, live_counts, pair_lists):
    block, windows, samples = traces.shape
    slots = pair_lists.shape[1]
    high, low = (jnp.asarray(t) for t in forward_tables())
    tiles = samples // LANES
    linear = traces.reshape(block, windows, tiles, LANES).transpose(0, 2, 1, 3)
    linear = linear.reshape(block * tiles * windows, LANES)
    vmem = pl.BlockSpec(memory_space=pltpu.VMEM)
    smem = pl.BlockSpec(memory_space=pltpu.SMEM)
    local = windows * block
    if routed:
        dma = pltpu.SemaphoreType.DMA
        hbm = pl.BlockSpec(memory_space=pltpu.MemorySpace.HBM)

        def in_hbm(value):
            return pltpu.with_memory_space_constraint(value, pltpu.MemorySpace.HBM)

        held = pl.pallas_call(
            functools.partial(gather_kernel, block, windows),
            out_shape=jax.ShapeDtypeStruct((win_total, chan_total, local, 2 * NF), jnp.float32),
            in_specs=[smem, hbm, hbm, hbm],
            out_specs=vmem,
            scratch_shapes=[
                pltpu.VMEM(linear.shape, linear.dtype),
                pltpu.VMEM(high.shape, high.dtype),
                pltpu.VMEM(low.shape, low.dtype),
                dma((3,)),
                dma((31,)),
                dma((16,)),
                dma((16,)),
            ],
            compiler_params=pltpu.CompilerParams(
                collective_id=0, has_side_effects=True, vmem_limit_bytes=24 * 2**20
            ),
            name="whiten_gather",
        )(live_counts, *(in_hbm(value) for value in (linear, high, low)))
    else:
        white = pl.pallas_call(
            functools.partial(white_kernel, block, windows),
            out_shape=jax.ShapeDtypeStruct((local, 2 * NF), jnp.float32),
            in_specs=[smem, vmem, vmem, vmem],
            out_specs=vmem,
            compiler_params=pltpu.CompilerParams(vmem_limit_bytes=24 * 2**20),
            name="whiten",
        )(live_counts, linear, high, low)
        held = lax.all_gather(white, ("win", "chan"), axis=0, tiled=False)
        held = held.reshape(win_total, chan_total, local, 2 * NF)
        held = jnp.take(held, pair_lists[0, :, :2].T.reshape(2 * slots), axis=1, mode="clip")

    firsts = block // win_total
    chunk = min(4, firsts)
    rows = chunk * block
    inv_high, inv_low = (jnp.asarray(t) for t in inverse_tables(windows * win_total))
    place = (lax.axis_index("win") * firsts).astype(jnp.int32).reshape(1)
    pairs = pair_lists.transpose(2, 0, 1)
    if not routed:
        places = jnp.arange(2 * slots, dtype=pairs.dtype).reshape(2, 1, slots)
        pairs = jnp.concatenate([places, pairs[2:]], axis=0)
    tall = slots * (NLAG // LANES)
    groups = firsts // chunk
    out = pl.pallas_call(
        functools.partial(lag_kernel, block, chunk, slots),
        out_shape=jax.ShapeDtypeStruct((firsts * block * tall, LANES), jnp.float32),
        in_specs=[smem, smem, vmem, vmem, vmem],
        out_specs=pl.BlockSpec(memory_space=pltpu.MemorySpace.HBM),
        scratch_shapes=[
            pltpu.VMEM((slots * rows, 2 * NF), jnp.bfloat16),
            pltpu.VMEM((slots * rows, 2 * NF), jnp.bfloat16),
            pltpu.VMEM((groups, rows * tall, LANES), jnp.float32),
            pltpu.SemaphoreType.DMA((groups,)),
        ],
        compiler_params=pltpu.CompilerParams(vmem_limit_bytes=32 * 2**20),
        name="cross_lags",
    )(pairs, place, held, inv_high, inv_low)
    out = out.reshape(firsts * block, NLAG // LANES, slots, LANES).transpose(0, 2, 1, 3)
    return out.reshape(firsts * block, slots, NLAG)


def solution(mesh):
    chan_total, win_total = mesh.shape["chan"], mesh.shape["win"]
    routed = (chan_total, win_total) == (16, 2)
    return jax.shard_map(
        functools.partial(body, routed, chan_total, win_total),
        mesh=mesh,
        in_specs=(P("chan", "win", None), P("chan"), P("chan", None, None)),
        out_specs=P("win", "chan", None),
        check_vma=False,
    )
```
